256 devices in a mesh: expert: 32 (over z, y_lo, core), tensor: 8 (over y_hi, x).
Axes of the slice: x: 4, y: 4 (y_hi: 2, y_lo: 2; y = y_hi * 2 + y_lo), z: 8, core: 2. Of those that a mesh axis runs over, the one named last changes fastest.
Arguments:
- tokens: bfloat16 [2048, 7168], P('expert', 'tensor'), may hold values from -6 to 6
- layer_output_gradient: bfloat16 [2048, 7168], P('expert', 'tensor'), may hold values from -6 to 6
- routes: int32 [2048, 2], P('expert'), may hold values from 0 to 31, all different within a row; in each aligned block of 64 rows (0 to 63, 64 to 127, ...) at most 8 rows name the same one
- router_weight_pair: float32 [2048, 2], P('expert'), may hold values from 0.05 to 1
- gating_projection: bfloat16 [32, 7168, 2432], P('expert', None, 'tensor'), may hold values from -0.0625 to 0.0625
- expanding_projection: bfloat16 [32, 7168, 2432], P('expert', None, 'tensor'), may hold values from -0.0625 to 0.0625
- contracting_projection: bfloat16 [32, 2432, 7168], P('expert', 'tensor'), may hold values from -0.125 to 0.125
- leading_correction_matrix: bfloat16 [32, 2432, 16], P('expert', 'tensor'), may hold values from -0.125 to 0.125
- trailing_correction_matrix: bfloat16 [32, 16, 7168], P('expert', None, 'tensor'), may hold values from -0.0625 to 0.0625
Outputs:
- source_derivative: bfloat16 [2048, 7168], P('expert', 'tensor')
- leading_correction_derivative: float32 [32, 2432, 16], P('expert', 'tensor')
- trailing_correction_derivative: float32 [32, 16, 7168], P('expert', None, 'tensor')
The draws below stay inside these ranges and needn't reach their ends.
Inputs may be any that keep to these rules, and one draw needn't show every extreme that they name: `routes`: among the 64 tokens of one index of expert no expert is named by more than 8 assignments, a bound that some block reaches.
All inputs are finite; a program needn't handle non-finite values.
Results may differ from the reference program's by a relative error of at most 0.019.
Values may be sent and summed in bfloat16 or wider, within the bound.
A program may use at most 128 MiB of HBM per device.

```python
import math
import jax
import jax.numpy as jnp
import numpy as np
from jax import lax

MODEL_WIDTH = 7168
HIDDEN_HALF = 2432
ADAPTER_RANK = 16
TOK_DEV = 64
CSRC = 8
EXPERT_COUNT = 32
TOKENS = 2048
N_EXPERT = 32


def steps_of(key, dims, shards, low, high):
    def one(axis_at, blocks):
        heights = jax.random.uniform(jax.random.fold_in(jax.random.fold_in(key, 6), axis_at), (blocks,), jnp.float32, low / len(shards), high / len(shards))
        return jnp.repeat(jnp.exp(heights), dims[axis_at] // blocks).reshape((-1,) + (1,) * (len(dims) - axis_at - 1))

    level = one(*shards[0])
    for cut in shards[1:]:
        level = level * one(*cut)
    return level


def routed_block(own_key, own, number, rows, count, top, most, lean):
    ranking = jax.random.permutation(own_key, count)
    heavy_load, ordinary = load_shares(count, rows * top, most, lean, True), load_shares(count, rows * top, most, lean, False)
    places = jnp.arange(count)

    def named(lengths, rotation):
        used = int((lengths > 0).sum())
        fixed = max(1, used // 4)
        shifted = fixed + (places - fixed + rotation * (used - fixed)) % max(1, count - fixed)
        return jnp.zeros((count,), jnp.int32).at[ranking[jnp.where(places < fixed, places, shifted)]].set(jnp.asarray(lengths, jnp.int32))

    lengths = jnp.where(number % 4 == 0, named(heavy_load, number // 4), named(ordinary, number - number // 4 - 1))
    mixed = jax.random.permutation(jax.random.fold_in(own, 3), count)
    donor, receiver = mixed[0:count // 2 * 2:2], mixed[1:count // 2 * 2:2]
    room = jnp.minimum(lengths[donor] - 1, most - lengths[receiver]) // 2
    room = jnp.where((donor == ranking[0]) | (receiver == ranking[0]) | (lengths[receiver] == 0), 0, jnp.maximum(room, 0))
    shifted = jax.random.randint(jax.random.fold_in(own, 4), (count // 2,), 0, 1 << 20) % (room + 1)
    lengths = lengths.at[donor].add(-shifted).at[receiver].add(shifted)
    labels = jnp.searchsorted(jnp.cumsum(lengths), jnp.arange(rows * top), side="right").astype(jnp.int32)
    listing = labels.reshape(top, rows).T
    listing = listing[jax.random.permutation(jax.random.fold_in(own, 1), rows)]
    rotation = jax.random.randint(jax.random.fold_in(own, 2), (rows, 1), 0, top)
    return jnp.take_along_axis(listing, (jnp.arange(top)[None, :] + rotation) % top, axis=1)


def load_shares(number_of, total, bound, slope, full):
    loads = [(1 << 20) // math.isqrt(rank ** slope) + 1 for rank in range(1, number_of + 1)]
    largest = bound if full else min(bound, max(-(-total // number_of), total * loads[0] // sum(loads)))
    least = 1 if total - largest >= number_of - 1 else 0
    counts, surplus = [largest] + [least] * (number_of - 1), total - largest - least * (number_of - 1)
    while surplus > 0:
        movable = [i for i in range(1, number_of) if counts[i] < largest] or [i for i in range(1, number_of) if counts[i] < bound]
        whole, budget = sum([loads[i] for i in movable]), surplus
        for i in movable:
            addition = min(bound - counts[i], max(1, budget * loads[i] // whole), surplus)
            counts[i] = counts[i] + addition
            surplus = surplus - addition
    return np.array(counts)


def centred(rng, shape, scale, bound, cuts=(), kind=jnp.bfloat16):
    result = jax.random.normal(rng, shape, jnp.float32) * scale
    if len(cuts) > 0:
        result = steps_of(rng, shape, cuts, -0.22, 0.18) * result
    return jnp.clip(result, min=-bound, max=bound).astype(kind)


def setup_inputs(seed: int = 0) -> dict:
    arg_keys = jax.random.split(jax.random.key(seed), 10)
    tokens = centred(arg_keys[0], (TOKENS, MODEL_WIDTH), 1.0, 6.0, ((0, 32), (1, 8)))
    layer_output_gradient = centred(arg_keys[1], (TOKENS, MODEL_WIDTH), 1.0, 6.0, ((0, 32), (1, 8)))
    routes_keys = jax.random.split(jax.random.fold_in(arg_keys[2], 1), TOKENS // TOK_DEV)
    routes_turns = jax.random.permutation(jax.random.fold_in(arg_keys[2], 3), TOKENS // TOK_DEV)
    routes = jax.vmap(lambda own, number: routed_block(jax.random.fold_in(arg_keys[2], 2), own, number, TOK_DEV, EXPERT_COUNT, 2, CSRC, 2))(routes_keys, routes_turns).reshape((TOKENS, 2))
    router_weight_pair = jnp.clip(jnp.exp(math.log(1.0) - 2.9957323 * jax.random.uniform(arg_keys[3], (TOKENS, 2), jnp.float32) ** steps_of(arg_keys[3], (TOKENS, 2), ((0, 32),), -0.2, 0.2)), 0.05, 1.0)
    gating_projection = centred(arg_keys[4], (EXPERT_COUNT, MODEL_WIDTH, HIDDEN_HALF), MODEL_WIDTH ** -0.5, 0.0625, ((0, 32), (2, 8)))
    expanding_projection = centred(arg_keys[5], (EXPERT_COUNT, MODEL_WIDTH, HIDDEN_HALF), MODEL_WIDTH ** -0.5, 0.0625, ((0, 32), (2, 8)))
    contracting_projection = centred(arg_keys[6], (EXPERT_COUNT, HIDDEN_HALF, MODEL_WIDTH), HIDDEN_HALF ** -0.5, 0.125, ((0, 32), (1, 8)))
    leading_correction_matrix = centred(arg_keys[7], (EXPERT_COUNT, HIDDEN_HALF, ADAPTER_RANK), HIDDEN_HALF ** -0.5, 0.125, ((0, 32), (1, 8)))
    trailing_correction_matrix = centred(arg_keys[8], (EXPERT_COUNT, ADAPTER_RANK, MODEL_WIDTH), MODEL_WIDTH ** -0.5, 0.0625, ((0, 32), (2, 8)))
    return dict(tokens=tokens, layer_output_gradient=layer_output_gradient, routes=routes, router_weight_pair=router_weight_pair, gating_projection=gating_projection, expanding_projection=expanding_projection, contracting_projection=contracting_projection, leading_correction_matrix=leading_correction_matrix, trailing_correction_matrix=trailing_correction_matrix)


correction_multiplier = 2.0


def group_rows(group_routes):
    flat = group_routes.reshape(-1)
    onehot = (flat[:, None] == jnp.arange(EXPERT_COUNT, dtype=jnp.int32)[None, :]).astype(jnp.int32)
    earlier = jnp.cumsum(onehot, axis=0) - onehot
    return jnp.sum(earlier * onehot, axis=1).astype(jnp.int32)


def reference(tokens, layer_output_gradient, routes, router_weight_pair, gating_projection, expanding_projection, contracting_projection, leading_correction_matrix, trailing_correction_matrix):
    per_group = routes.reshape(N_EXPERT, TOK_DEV, 2)
    slots = jax.vmap(group_rows)(per_group)
    group_ids = jnp.arange(N_EXPERT, dtype=jnp.int32)[:, None]
    rows = per_group.reshape(N_EXPERT, -1) * (N_EXPERT * CSRC) + group_ids * CSRC + slots
    rows = rows.reshape(-1).astype(jnp.int32)
    total = EXPERT_COUNT * N_EXPERT * CSRC
    token_rows = jnp.repeat(tokens, 2, axis=0)
    scaled = (router_weight_pair[:, :, None] * layer_output_gradient[:, None, :].astype(jnp.float32)).astype(jnp.bfloat16).reshape(-1, MODEL_WIDTH)
    source_token_entries = jnp.zeros((total, MODEL_WIDTH), jnp.bfloat16).at[rows].set(token_rows).reshape(EXPERT_COUNT, N_EXPERT * CSRC, MODEL_WIDTH)
    routing_weighted_entries = jnp.zeros((total, MODEL_WIDTH), jnp.bfloat16).at[rows].set(scaled).reshape(EXPERT_COUNT, N_EXPERT * CSRC, MODEL_WIDTH)

    def specialist_index(items):
        x_rows, output_grad_rows, wg, wu, down_matrix, first_adapter_act, fb = items
        gate = jnp.dot(x_rows, wg, preferred_element_type=jnp.float32)
        up = jnp.dot(x_rows, wu, preferred_element_type=jnp.float32)
        sig = jax.nn.sigmoid(gate)
        act = gate * sig
        hidden_units = (act * up).astype(jnp.bfloat16)
        lowrank_rows = jnp.dot(hidden_units, first_adapter_act, preferred_element_type=jnp.float32).astype(jnp.bfloat16)
        probe_vector = jnp.dot(output_grad_rows, fb.T, preferred_element_type=jnp.float32).astype(jnp.bfloat16)
        hidden_gradient = jnp.dot(output_grad_rows, down_matrix.T, preferred_element_type=jnp.float32) + correction_multiplier * jnp.dot(probe_vector, first_adapter_act.T, preferred_element_type=jnp.float32)
        dgate = (hidden_gradient * up * sig * (1.0 + gate * (1.0 - sig))).astype(jnp.bfloat16)
        dup = (hidden_gradient * act).astype(jnp.bfloat16)
        first_factor_gradient = correction_multiplier * jnp.dot(hidden_units.T, probe_vector, preferred_element_type=jnp.float32)
        second_factor_gradient = correction_multiplier * jnp.dot(lowrank_rows.T, output_grad_rows, preferred_element_type=jnp.float32)
        source_derivative_entries = jnp.dot(dgate, wg.T, preferred_element_type=jnp.float32) + jnp.dot(dup, wu.T, preferred_element_type=jnp.float32)
        return source_derivative_entries, first_factor_gradient, second_factor_gradient

    source_derivative_entries, leading_correction_derivative, trailing_correction_derivative = lax.map(specialist_index, (source_token_entries, routing_weighted_entries, gating_projection, expanding_projection, contracting_projection, leading_correction_matrix, trailing_correction_matrix))
    picked = source_derivative_entries.reshape(total, MODEL_WIDTH)[rows].reshape(TOKENS, 2, MODEL_WIDTH)
    source_derivative = (picked[:, 0] + picked[:, 1]).astype(jnp.bfloat16)
    return source_derivative, leading_correction_derivative, trailing_correction_derivative
```

```python
import functools

import jax
import jax.numpy as jnp
from jax import lax
from jax.experimental import pallas as pl
from jax.experimental.pallas import tpu as pltpu
from jax.sharding import PartitionSpec as P

MESH = pl.DeviceIdType.MESH
F32, BF16 = jnp.float32, jnp.bfloat16
NT = (((1,), (1,)), ((), ()))
TN = (((0,), (0,)), ((), ()))

CSRC = 8
GROUPS = 32
HALF = 16
ROWS = HALF * CSRC
WIDTH = 896
TWIDE = 8
SCALE = 2.0
DZ = (0, 1, 7, 2, 6, 3, 5, 4)

N_A, N_B = 9, 7
A1, A2, B1, B2 = (0, 5), (5, 4), (9, 4), (13, 3)
A, B = (0, N_A), (N_A, N_B)


def dot(a, b, dims=(((1,), (0,)), ((), ()))):
    return lax.dot_general(a, b, dims, preferred_element_type=F32)


def kernel(
    tok, grad, routes, weights, wg_hbm, wu_hbm, wd_hbm, lead, trail,
    out, lead_out, trail_out,
    wg, wu, wd, held, sendbuf, acc_g, acc_u, acc_d, hid, dgate, dup, probe,
    low_mine, low_all, x2s, to_r, to_l, to_y, x2_l, x2_r, from_l, from_r, from_y, own_sum,
    ret_out, ret_in, pick,
    w_sem, a2a_s, a2a_r, b_s, b_r, ag_s, ag_r, rs_s, rs_r, low_s, low_r, ret_s, ret_r, loc_sem,
):
    e = lax.axis_index("expert")
    t = lax.axis_index("tensor")
    z, yl, c = e // 4, (e // 2) % 2, e % 2
    yh, x = t // 4, t % 4
    xr, xl, x2, yo = (x + 1) % 4, (x + 3) % 4, (x + 2) % 4, 1 - yh
    to_right, to_left, across = (e, yh * 4 + xr), (e, yh * 4 + xl), (e, yo * 4 + x)
    col = {"o": x, "r": xr, "l": xl, "2": x2}
    ch = {k: yh * 4 + v for k, v in col.items()}
    ch.update({"p" + k: yo * 4 + v for k, v in col.items()})

    def expert_at(p, sign):
        dz, dyl, dc = DZ[p // 4], (p // 2) % 2, p % 2
        zz = (z + (dz if sign > 0 else 8 - dz)) % 8
        yy = 1 - yl if dyl else yl
        cc = 1 - c if dc else c
        return (zz * 4 + yy * 2 + cc, t)

    peers = [(e, (t + k) % TWIDE) for k in range(1, TWIDE)]

    w_copies = [
        pltpu.make_async_copy(wg_hbm.at[0], wg, w_sem.at[0]),
        pltpu.make_async_copy(wu_hbm.at[0], wu, w_sem.at[1]),
    ]
    for j in range(TWIDE):
        w_copies.append(
            pltpu.make_async_copy(
                wd_hbm.at[0, :, pl.ds(j * WIDTH, WIDTH)], wd.at[j, pl.ds(0, 304)], w_sem.at[2 + j]
            )
        )
    w_copies.append(
        pltpu.make_async_copy(trail.at[0], wd.at[t, pl.ds(304, 16)], w_sem.at[10])
    )

    barrier = pltpu.get_barrier_semaphore()
    for p in range(1, GROUPS):
        pl.semaphore_signal(barrier, inc=1, device_id=expert_at(p, 1), device_id_type=MESH)
    for peer in peers:
        pl.semaphore_signal(barrier, inc=1, device_id=peer, device_id_type=MESH)
    for cp in w_copies:
        cp.start()

    r = routes[...]
    experts = lax.broadcasted_iota(jnp.int32, (64, GROUPS), 1)
    hot = [(r[:, k : k + 1] == experts).astype(F32) for k in range(2)]
    lower = (
        lax.broadcasted_iota(jnp.int32, (64, 64), 0) > lax.broadcasted_iota(jnp.int32, (64, 64), 1)
    ).astype(BF16)
    earlier = dot(lower, (hot[0] + hot[1]).astype(BF16))
    lanes = lax.broadcasted_iota(jnp.int32, (64, GROUPS * CSRC), 1)
    picks, scaled = [], []
    grads = grad[...].astype(F32)
    for k in range(2):
        rk = r[:, k : k + 1]
        dz = ((rk >> 2) - z) & 7
        near = jnp.where(dz == 0, 0, jnp.where(dz <= 4, 2 * dz - 1, 16 - 2 * dz))
        place = near * 4 + (((rk >> 1) & 1) ^ yl) * 2 + ((rk & 1) ^ c)
        slot = jnp.sum(earlier * hot[k], axis=1, keepdims=True).astype(jnp.int32)
        picks.append(((place * CSRC + slot) == lanes).astype(F32))
        scaled.append((weights[:, k : k + 1] * grads).astype(BF16))
    both = (picks[0] + picks[1]).astype(BF16)
    pick[...] = both
    xs = dot(both, tok[...], TN)
    gs = dot(picks[0].astype(BF16), scaled[0], TN) + dot(picks[1].astype(BF16), scaled[1], TN)
    packed = jnp.concatenate(
        [xs.reshape(GROUPS, CSRC, WIDTH), gs.reshape(GROUPS, CSRC, WIDTH)], axis=1
    ).astype(BF16)
    sendbuf[...] = packed

    pl.semaphore_wait(barrier, GROUPS - 1 + len(peers))

    started = []

    def remote(src, dst, ss, rs, dev):
        return pltpu.make_async_remote_copy(
            src_ref=src, dst_ref=dst, send_sem=ss, recv_sem=rs, device_id=dev, device_id_type=MESH
        )

    def send(*args):
        cp = remote(*args)
        cp.start()
        started.append(cp)

    def arrive(dst, ss, rs):
        remote(dst, dst, ss, rs, to_right).wait_recv()

    own_copy = pltpu.make_async_copy(sendbuf.at[0], held.at[t, 0], loc_sem.at[0])
    own_copy.start()
    for p in range(1, GROUPS):
        send(sendbuf.at[p], held.at[t, p], a2a_s.at[p], a2a_r.at[p], expert_at(p, 1))
    for k, peer in enumerate(peers):
        send(trail.at[0], wd.at[t, pl.ds(304, 16)], b_s.at[k], b_r.at[k], peer)

    def region(name, h, part):
        return held.at[ch[name], pl.ds(h * HALF + part[0], part[1])]

    def forward(h, i, name, part, dev):
        ref = region(name, h, part)
        send(ref, ref, ag_s.at[h, i], ag_r.at[h, i], dev)

    def got(h, i, name, part):
        arrive(region(name, h, part), ag_s.at[h, i], ag_r.at[h, i])

    def products(h, name, first=False):
        j = ch[name]
        block = held[j, pl.ds(h * HALF, HALF)].astype(F32)
        xrows = block[:, :CSRC].reshape(ROWS, WIDTH).astype(BF16)
        grows = block[:, CSRC:].reshape(ROWS, WIDTH).astype(BF16)
        rows = pl.ds(pl.multiple_of(j * WIDTH, WIDTH), WIDTH)
        for acc, val in (
            (acc_g, dot(xrows, wg[rows, :])),
            (acc_u, dot(xrows, wu[rows, :])),
            (acc_d, dot(grows, wd[j], NT)),
        ):
            if first:
                acc[h] = val
            else:
                acc[h] += val

    def input_part(h, name):
        j = ch[name]
        rows = pl.ds(pl.multiple_of(j * WIDTH, WIDTH), WIDTH)
        return dot(dgate[h], wg[rows, :], NT) + dot(dup[h], wu[rows, :], NT)

    def middle(h):
        probe_h = acc_d[h][:, 304:320].astype(BF16)
        probe[h] = probe_h
        gate, up = acc_g[h], acc_u[h]
        dh = acc_d[h][:, :304] + SCALE * dot(probe_h, lead[0], NT)
        sig = jax.nn.sigmoid(gate)
        act = gate * sig
        hidden = (act * up).astype(BF16)
        hid[h] = hidden
        dgate[h] = (dh * up * sig * (1.0 + gate * (1.0 - sig))).astype(BF16)
        dup[h] = (dh * act).astype(BF16)
        low_mine[h] = jnp.transpose(dot(hidden, lead[0]))

    def half(h):
        if h == 0:
            own_copy.wait()
        for p in range(max(1, h * HALF), (h + 1) * HALF):
            arrive(held.at[t, p], a2a_s.at[p], a2a_r.at[p])
        forward(h, 0, "o", A, across)
        forward(h, 1, "o", B, to_right)
        forward(h, 2, "o", B, to_left)
        forward(h, 4, "o", A, to_right)
        forward(h, 5, "o", A, to_left)
        forward(h, 3, "o", B, across)
        yield
        if h == 0:
            for cp in w_copies:
                cp.wait()
        products(h, "o", first=True)
        yield
        got(h, 1, "l", B)
        forward(h, 6, "l", B1, to_right)
        forward(h, 8, "l", B, across)
        got(h, 2, "r", B)
        forward(h, 7, "r", B2, to_left)
        forward(h, 9, "r", B, across)
        got(h, 0, "po", A)
        forward(h, 14, "po", A, to_right)
        forward(h, 15, "po", A, to_left)
        yield
        got(h, 4, "l", A)
        forward(h, 12, "l", A1, to_right)
        got(h, 5, "r", A)
        forward(h, 13, "r", A2, to_left)
        yield
        if h == 0:
            for k in range(TWIDE - 1):
                arrive(wd.at[(t + TWIDE - 1 - k) % TWIDE, pl.ds(304, 16)], b_s.at[k], b_r.at[k])
        products(h, "l")
        yield
        got(h, 6, "2", B1)
        forward(h, 10, "2", B1, across)
        got(h, 7, "2", B2)
        forward(h, 11, "2", B2, across)
        yield
        products(h, "r")
        yield
        got(h, 14, "pl", A)
        forward(h, 16, "pl", A1, to_right)
        got(h, 15, "pr", A)
        forward(h, 17, "pr", A2, to_left)
        yield
        got(h, 12, "2", A1)
        got(h, 13, "2", A2)
        products(h, "2")
        yield
        got(h, 3, "po", B)
        products(h, "po")
        yield
        got(h, 8, "pl", B)
        products(h, "pl")
        yield
        got(h, 9, "pr", B)
        products(h, "pr")
        yield
        got(h, 16, "p2", A1)
        got(h, 17, "p2", A2)
        got(h, 10, "p2", B1)
        got(h, 11, "p2", B2)
        products(h, "p2")
        yield
        middle(h)
        yield
        for s, row in ((1, "p"), (0, "")):
            x2s[h, s] = input_part(h, row + "2").astype(BF16)
            send(x2s.at[h, s, pl.ds(0, 64)], x2_l.at[h, s], rs_s.at[h, s, 0], rs_r.at[h, s, 0], to_right)
            send(x2s.at[h, s, pl.ds(64, 64)], x2_r.at[h, s], rs_s.at[h, s, 1], rs_r.at[h, s, 1], to_left)
            yield
        for k, peer in enumerate(peers):
            send(low_mine.at[h], low_all.at[h, k], low_s.at[h, k], low_r.at[h, k], peer)
        for s, row in ((1, "p"), (0, "")):
            part = input_part(h, row + "r")
            arrive(x2_l.at[h, s], rs_s.at[h, s, 0], rs_r.at[h, s, 0])
            to_r[h, s] = jnp.concatenate(
                [part[:64] + x2_l[h, s].astype(F32), part[64:]], axis=0
            ).astype(BF16)
            send(to_r.at[h, s], from_l.at[h, s], rs_s.at[h, s, 2], rs_r.at[h, s, 2], to_right)
            yield
            part = input_part(h, row + "l")
            arrive(x2_r.at[h, s], rs_s.at[h, s, 1], rs_r.at[h, s, 1])
            to_l[h, s] = jnp.concatenate(
                [part[:64], part[64:] + x2_r[h, s].astype(F32)], axis=0
            ).astype(BF16)
            send(to_l.at[h, s], from_r.at[h, s], rs_s.at[h, s, 3], rs_r.at[h, s, 3], to_left)
            yield
        own_sum[1] = input_part(h, "po")
        own_sum[0] = input_part(h, "o")
        for s in (1, 0):
            arrive(from_l.at[h, s], rs_s.at[h, s, 2], rs_r.at[h, s, 2])
            arrive(from_r.at[h, s], rs_s.at[h, s, 3], rs_r.at[h, s, 3])
            total = own_sum[s] + from_l[h, s].astype(F32) + from_r[h, s].astype(F32)
            if s:
                to_y[h] = total.astype(BF16)
                send(to_y.at[h], from_y.at[h], rs_s.at[h, s, 4], rs_r.at[h, s, 4], across)
            else:
                own_sum[0] = total
        arrive(from_y.at[h], rs_s.at[h, 1, 4], rs_r.at[h, 1, 4])
        final = (own_sum[0] + from_y[h].astype(F32)).reshape(HALF, CSRC, WIDTH)
        ret_out[pl.ds(h * HALF, HALF)] = jnp.concatenate(
            [final[:, :, :512], final[:, :, 384:]], axis=1
        ).astype(BF16)
        for p in range(max(1, h * HALF), (h + 1) * HALF):
            send(ret_out.at[p], ret_in.at[p], ret_s.at[p], ret_r.at[p], expert_at(p, -1))
        yield

    order = [0] * 9 + [1] * 1 + [0] * 4 + [1] * 2 + [0] * 2
    order += [1, 0, 1, 0, 1, 0, 1, 0, 1, 0, 1, 0]
    gens = [half(0), half(1)]
    for h in order:
        next(gens[h], None)
    for g in gens:
        for _ in g:
            pass

    lead_out[0] = SCALE * (dot(hid[0], probe[0], TN) + dot(hid[1], probe[1], TN))
    own = held[t].astype(F32)
    trail_sum = jnp.zeros((16, WIDTH), F32)
    for h in range(2):
        low = low_mine[h]
        for k in range(TWIDE - 1):
            arrive(low_all.at[h, k], low_s.at[h, k], low_r.at[h, k])
            low = low + low_all[h, k]
        grows = own[h * HALF : (h + 1) * HALF, CSRC:].reshape(ROWS, WIDTH).astype(BF16)
        trail_sum = trail_sum + dot(low.astype(BF16), grows)
    trail_out[0] = SCALE * trail_sum

    for p in range(1, GROUPS):
        arrive(ret_in.at[p], ret_s.at[p], ret_r.at[p])
    ret_in[0] = ret_out[0]
    back = ret_in[...].astype(F32)
    first = back[:, :CSRC].reshape(GROUPS * CSRC, 512).astype(BF16)
    last = back[:, CSRC:].reshape(GROUPS * CSRC, 512).astype(BF16)
    out[:, 0:512] = dot(pick[...], first).astype(BF16)
    out[:, 512:WIDTH] = dot(pick[...], last)[:, 128:].astype(BF16)

    for cp in started:
        cp.wait_send()


def on_device(tok, grad, routes, weights, wg, wu, wd, lead, trail):
    vm = pl.BlockSpec(memory_space=pltpu.VMEM)
    hbm = pl.BlockSpec(memory_space=pl.ANY)
    dma = pltpu.SemaphoreType.DMA
    return pl.pallas_call(
        kernel,
        out_shape=(
            jax.ShapeDtypeStruct((64, WIDTH), BF16),
            jax.ShapeDtypeStruct((1, 304, 16), F32),
            jax.ShapeDtypeStruct((1, 16, WIDTH), F32),
        ),
        in_specs=[vm, vm, vm, vm, hbm, hbm, hbm, vm, vm],
        out_specs=(vm, vm, vm),
        scratch_shapes=[
            pltpu.VMEM((7168, 304), BF16),
            pltpu.VMEM((7168, 304), BF16),
            pltpu.VMEM((TWIDE, 320, WIDTH), BF16),
            pltpu.VMEM((TWIDE, GROUPS, 16, WIDTH), BF16),
            pltpu.VMEM((GROUPS, 16, WIDTH), BF16),
            pltpu.VMEM((2, ROWS, 304), F32),
            pltpu.VMEM((2, ROWS, 304), F32),
            pltpu.VMEM((2, ROWS, 320), F32),
            pltpu.VMEM((2, ROWS, 304), BF16),
            pltpu.VMEM((2, ROWS, 304), BF16),
            pltpu.VMEM((2, ROWS, 304), BF16),
            pltpu.VMEM((2, ROWS, 16), BF16),
            pltpu.VMEM((2, 16, ROWS), F32),
            pltpu.VMEM((2, TWIDE - 1, 16, ROWS), F32),
            pltpu.VMEM((2, 2, ROWS, WIDTH), BF16),
            pltpu.VMEM((2, 2, ROWS, WIDTH), BF16),
            pltpu.VMEM((2, 2, ROWS, WIDTH), BF16),
            pltpu.VMEM((2, ROWS, WIDTH), BF16),
            pltpu.VMEM((2, 2, 64, WIDTH), BF16),
            pltpu.VMEM((2, 2, 64, WIDTH), BF16),
            pltpu.VMEM((2, 2, ROWS, WIDTH), BF16),
            pltpu.VMEM((2, 2, ROWS, WIDTH), BF16),
            pltpu.VMEM((2, ROWS, WIDTH), BF16),
            pltpu.VMEM((2, ROWS, WIDTH), F32),
            pltpu.VMEM((GROUPS, 16, 512), BF16),
            pltpu.VMEM((GROUPS, 16, 512), BF16),
            pltpu.VMEM((64, GROUPS * CSRC), BF16),
            dma((11,)),
            dma((GROUPS,)),
            dma((GROUPS,)),
            dma((TWIDE - 1,)),
            dma((TWIDE - 1,)),
            dma((2, 18)),
            dma((2, 18)),
            dma((2, 2, 5)),
            dma((2, 2, 5)),
            dma((2, TWIDE - 1)),
            dma((2, TWIDE - 1)),
            dma((GROUPS,)),
            dma((GROUPS,)),
            dma((1,)),
        ],
        compiler_params=pltpu.CompilerParams(
            collective_id=0, has_side_effects=True, vmem_limit_bytes=56 * 1024 * 1024
        ),
        cost_estimate=pl.CostEstimate(
            flops=6_000_000_000, bytes_accessed=16_000_000, transcendentals=80_000
        ),
    )(tok, grad, routes, weights, wg, wu, wd, lead, trail)


def solution(mesh):
    placed = (
        P("expert", "tensor"),
        P("expert", "tensor"),
        P("expert", None),
        P("expert", None),
        P("expert", None, "tensor"),
        P("expert", None, "tensor"),
        P("expert", "tensor", None),
        P("expert", "tensor", None),
        P("expert", None, "tensor"),
    )
    return jax.shard_map(
        on_device,
        mesh=mesh,
        in_specs=placed,
        out_specs=(P("expert", "tensor"), P("expert", "tensor", None), P("expert", None, "tensor")),
        check_vma=False,
    )
```

```python
import functools

import jax
import jax.numpy as jnp
from jax import lax
from jax.experimental import pallas as pl
from jax.experimental.pallas import tpu as pltpu
from jax.sharding import PartitionSpec as P

MESH = pl.DeviceIdType.MESH
F32, BF16 = jnp.float32, jnp.bfloat16
NT = (((1,), (1,)), ((), ()))
TN = (((0,), (0,)), ((), ()))

CSRC = 8
GROUPS = 32
PARTS = 4
GPART = GROUPS // PARTS
ROWS = GPART * CSRC
WIDTH = 896
UNITS = 304
RANK = 16
TWIDE = 8
SCALE = 2.0


def pair(m, dc):
    return tuple((dz, dyl, dc) for dz in (m, 8 - m) for dyl in range(2))


PLACES = (
    tuple((0, p // 2, p % 2) for p in range(4))
    + sum((pair(m, dc) for m in (1, 2, 3) for dc in range(2)), ())
    + tuple((4, p // 2, p % 2) for p in range(4))
)

CUTS = ((3, 3, 1, 1), (3, 3, 1, 1), (3, 3, 1, 1), (3, 3, 1, 1))


def cut(i, key):
    b1, b2, a1, a2 = CUTS[i][2], CUTS[i][3], CUTS[i][0], CUTS[i][1]
    b = b1 + b2
    at, n = {
        "B1": (0, b1), "B2": (b1, b2), "B": (0, b), "A1": (b, a1), "A2": (b + a1, a2), "A": (b, a1 + a2),
    }[key]
    return i * GPART + at, n


GATHER = (
    ("o", "A", "y", "po"), ("o", "B", "r", "l"), ("o", "B", "l", "r"), ("o", "B", "y", "po"),
    ("o", "A", "r", "l"), ("o", "A", "l", "r"), ("l", "B1", "r", "2"), ("r", "B2", "l", "2"),
    ("l", "B", "y", "pl"), ("r", "B", "y", "pr"), ("2", "B1", "y", "p2"), ("2", "B2", "y", "p2"),
    ("l", "A1", "r", "2"), ("r", "A2", "l", "2"), ("po", "A", "r", "pl"), ("po", "A", "l", "pr"),
    ("pl", "A1", "r", "p2"), ("pr", "A2", "l", "p2"),
)
STEPS = {
    "g0": ((), (1, 2, 3)), "g1": ((), (0, 4, 5)), "g2": ((1,), (6, 8)), "g3": ((2,), (7, 9)),
    "g4": ((0,), (14, 15)), "g5": ((4,), (12,)), "g6": ((5,), (13,)), "g7": ((6,), (10,)),
    "g8": ((7,), (11,)), "g9": ((14,), (16,)), "g10": ((15,), (17,)),
}
CHUNKS = {
    "o": (), "l": (1, 4), "r": (2, 5), "2": (6, 7, 12, 13), "po": (0, 3), "pl": (14, 8), "pr": (15, 9),
    "p2": (16, 17, 10, 11),
}
SUMS = (
    ("p2", 0, 16, "r"), ("p2", 16, 16, "l"), ("p2", 32, 32, "y"), ("pr", 32, 32, "y"), ("pl", 32, 32, "y"),
    ("po", 32, 32, "y"), ("pr", 0, 32, "r"), ("pl", 0, 32, "l"), ("po", 0, 32, "y"), ("2", 0, 32, "r"),
    ("2", 32, 32, "l"), ("r", 0, 32, "r"), ("l", 0, 32, "l"), ("r", 32, 32, "r"), ("l", 32, 32, "l"),
)
MAKE = {"p2": (0, 1, 2), "pr": (3,), "pl": (4,), "po": (5,), "2": (9,), "l": (12,), "r": (), "o": ()}
ADDS = {
    "s0": ((0,), 6), "s1": ((1,), 7), "s2": ((6, 7), 8), "s3": ((2,), 10), "s4": ((9,), 11), "s5": ((3,), 13),
    "s6": ((10, 4), 14),
}
LAST = (5, 8, 11, 12, 13, 14)

NAMES = tuple(CHUNKS)

ORDER = (
    (0, "g0"), (0, "g1"), (0, "co"), (1, "g0"), (1, "g1"), (1, "co"), (0, "g2"), (0, "g3"), (0, "g4"),
    (0, "g5"), (0, "g6"), (0, "cl"), (0, "cpo"), (1, "g2"), (1, "g3"), (0, "cr"), (1, "g4"), (1, "g5"),
    (1, "g6"), (1, "cpo"), (0, "g7"), (0, "g8"), (2, "g0"), (2, "g1"), (1, "cr"), (1, "cl"), (2, "co"),
    (0, "g9"), (0, "g10"), (0, "cpl"), (0, "cpr"), (0, "c2"), (1, "g7"), (1, "g8"), (3, "g0"), (3, "g1"),
    (3, "co"), (1, "g9"), (1, "g10"), (1, "cpl"), (2, "g4"), (1, "cpr"), (2, "cpo"), (1, "c2"), (2, "g2"),
    (2, "g3"), (2, "g5"), (2, "g6"), (3, "g4"), (2, "cl"), (2, "cr"), (3, "cpo"), (0, "cp2"), (0, "mid"),
    (0, "dp2"), (3, "g2"), (3, "g3"), (0, "dpr"), (0, "dpl"), (0, "dpo"), (0, "d2"), (0, "dr"), (0, "dl"),
    (0, "do"), (0, "s3"), (3, "g5"), (3, "g6"), (3, "cr"), (3, "cl"), (1, "cp2"), (1, "mid"), (0, "s5"),
    (1, "dp2"), (1, "dpr"), (1, "dpl"), (1, "dpo"), (1, "d2"), (1, "dr"), (1, "dl"), (1, "do"), (2, "g9"),
    (2, "g10"), (2, "cpl"), (2, "g7"), (2, "g8"), (1, "s3"), (2, "cpr"), (1, "s5"), (2, "c2"), (3, "g9"),
    (3, "g10"), (3, "cpl"), (0, "s1"), (0, "s0"), (3, "g7"), (3, "g8"), (3, "cpr"), (0, "s4"), (0, "s6"),
    (3, "c2"), (1, "s1"), (1, "s0"), (1, "s4"), (2, "cp2"), (2, "mid"), (2, "dp2"), (2, "dpr"), (1, "s6"),
    (2, "dpl"), (2, "dpo"), (2, "d2"), (2, "dr"), (2, "dl"), (2, "do"), (3, "cp2"), (2, "s3"), (0, "s2"),
    (3, "mid"), (3, "dp2"), (2, "s5"), (3, "dpr"), (3, "dpl"), (3, "dpo"), (3, "d2"), (3, "dr"), (1, "s2"),
    (3, "dl"), (2, "s1"), (3, "do"), (2, "s0"), (0, "end"), (2, "s4"), (3, "s3"), (3, "s0"), (2, "s6"),
    (3, "s5"), (3, "s1"), (3, "s4"), (2, "s2"), (1, "end"), (3, "s6"), (2, "end"), (3, "s2"), (3, "end"),
)


def dot(a, b, dims=(((1,), (0,)), ((), ()))):
    return lax.dot_general(a, b, dims, preferred_element_type=F32)


def kernel(
    tok, grad, routes, weights, wg_hbm, wu_hbm, wd_hbm, lead, trail,
    out, lead_out, trail_out,
    wgu, wd, held, sendbuf, acc_x, acc_d, hid, dboth, probe, low_mine, low_all, part_sum,
    sum_out, sum_in, ret_out, ret_in, pick,
    w_sem, a2a_s, a2a_r, b_s, b_r, ag_s, ag_r, rs_s, rs_r, low_s, low_r, ret_s, ret_r, loc_sem,
):
    e = lax.axis_index("expert")
    t = lax.axis_index("tensor")
    z, yl, c = e // 4, (e // 2) % 2, e % 2
    yh, x = t // 4, t % 4
    xr, xl, x2, yo = (x + 1) % 4, (x + 3) % 4, (x + 2) % 4, 1 - yh
    way = {"r": (e, yh * 4 + xr), "l": (e, yh * 4 + xl), "y": (e, yo * 4 + x)}
    col = {"o": x, "r": xr, "l": xl, "2": x2}
    ch = {k: yh * 4 + v for k, v in col.items()}
    ch.update({"p" + k: yo * 4 + v for k, v in col.items()})

    def expert_at(p, sign):
        dz, dyl, dc = PLACES[p]
        zz = (z + (dz if sign > 0 else 8 - dz)) % 8
        yy = 1 - yl if dyl else yl
        cc = 1 - c if dc else c
        return (zz * 4 + yy * 2 + cc, t)

    peers = [(e, (t + k) % TWIDE) for k in range(1, TWIDE)]

    w_copies = []
    for j in range(TWIDE):
        cols = pl.ds(j * WIDTH, WIDTH)
        for i, (src, dst, at) in enumerate(((wg_hbm, wgu, 0), (wu_hbm, wgu, UNITS), (wd_hbm, wd, 0))):
            w_copies.append(
                pltpu.make_async_copy(
                    src.at[0, :, cols], dst.at[j, pl.ds(at, UNITS)], w_sem.at[i, j]
                )
            )
    w_copies.append(
        pltpu.make_async_copy(trail.at[0], wd.at[t, pl.ds(UNITS, RANK)], loc_sem.at[1])
    )

    barrier = pltpu.get_barrier_semaphore()
    for p in range(1, GROUPS):
        pl.semaphore_signal(barrier, inc=1, device_id=expert_at(p, 1), device_id_type=MESH)
    for peer in peers:
        pl.semaphore_signal(barrier, inc=1, device_id=peer, device_id_type=MESH)
    for cp in w_copies:
        cp.start()

    experts = lax.broadcasted_iota(jnp.int32, (GROUPS, 64), 0)
    hot = [(routes[k : k + 1, :] == experts).astype(F32) for k in range(2)]
    upper = (
        lax.broadcasted_iota(jnp.int32, (64, 64), 0) < lax.broadcasted_iota(jnp.int32, (64, 64), 1)
    ).astype(BF16)
    earlier = dot((hot[0] + hot[1]).astype(BF16), upper)
    slots = lax.broadcasted_iota(jnp.int32, (GROUPS * CSRC, 64), 0)
    picks = []
    for k in range(2):
        rk = routes[k : k + 1, :]
        dz = ((rk >> 2) - z) & 7
        dyl, dc = ((rk >> 1) & 1) ^ yl, (rk & 1) ^ c
        m = jnp.minimum(dz, 8 - dz)
        place = jnp.where(
            m % 4 == 0,
            m * 7 + dyl * 2 + dc,
            m * 8 - 4 + dc * 4 + jnp.where(dz > 4, 2, 0) + dyl,
        )
        slot = jnp.sum(earlier * hot[k], axis=0, keepdims=True).astype(jnp.int32)
        picks.append(((place * CSRC + slot) == slots).astype(F32))
    both = (picks[0] + picks[1]).astype(BF16)
    pick[...] = both
    xs = dot(both, tok[...])
    factor = picks[0] * weights[0:1, :] + picks[1] * weights[1:2, :]
    gs = jnp.sum(factor, axis=1, keepdims=True) * dot(both, grad[...])
    packed = jnp.concatenate(
        [xs.reshape(GROUPS, CSRC, WIDTH), gs.reshape(GROUPS, CSRC, WIDTH)], axis=1
    ).astype(BF16)
    sendbuf[...] = packed

    pl.semaphore_wait(barrier, GROUPS - 1 + len(peers))

    started = []

    def remote(src, dst, ss, rs, dev):
        return pltpu.make_async_remote_copy(
            src_ref=src, dst_ref=dst, send_sem=ss, recv_sem=rs, device_id=dev, device_id_type=MESH
        )

    def send(*args):
        cp = remote(*args)
        cp.start()
        started.append(cp)

    def arrive(dst, ss, rs):
        remote(dst, dst, ss, rs, way["y"]).wait_recv()

    def exchange(groups):
        for p in groups:
            send(sendbuf.at[p], held.at[t, p], a2a_s.at[p], a2a_r.at[p], expert_at(p, 1))

    own_copy = pltpu.make_async_copy(sendbuf.at[0], held.at[t, 0], loc_sem.at[0])
    own_copy.start()
    exchange(range(1, 2 * GPART))

    done = set()

    def once(key):
        new = key not in done
        done.add(key)
        return new

    def have_own(i, key):
        at, n = cut(i, key)
        for p in range(at, at + n):
            if p and once(("own", p)):
                arrive(held.at[t, p], a2a_s.at[p], a2a_r.at[p])
        if i == 0 and once("copied"):
            own_copy.wait()

    def region(name, i, key):
        at, n = cut(i, key)
        return held.at[ch[name], pl.ds(at, n)]

    def gather_step(i, step):
        needs, sends = STEPS[step]
        if step in ("g0", "g1"):
            have_own(i, "B" if step == "g0" else "A")
        gathered(i, needs)
        for m in sends:
            name, key, to, _ = GATHER[m]
            ref = region(name, i, key)
            send(ref, ref, ag_s.at[i, m], ag_r.at[i, m], way[to])
        if step == "g1" and i == 0:
            exchange(range(2 * GPART, GROUPS))
            for k, peer in enumerate(peers):
                send(trail.at[0], wd.at[t, pl.ds(UNITS, RANK)], b_s.at[k], b_r.at[k], peer)

    def gathered(i, needs):
        for m in needs:
            if once(("g", i, m)):
                arrive(region(GATHER[m][3], i, GATHER[m][1]), ag_s.at[i, m], ag_r.at[i, m])

    def products(i, name):
        gathered(i, CHUNKS[name])
        if once("weights"):
            for cp in w_copies:
                cp.wait()
        if name != "o" and once("adapter"):
            for k in range(TWIDE - 1):
                arrive(wd.at[(t + TWIDE - 1 - k) % TWIDE, pl.ds(UNITS, RANK)], b_s.at[k], b_r.at[k])
        j = ch[name]
        block = held[j, pl.ds(i * GPART, GPART)].astype(F32)
        xrows = block[:, :CSRC].reshape(ROWS, WIDTH).astype(BF16)
        grows = block[:, CSRC:].reshape(ROWS, WIDTH).astype(BF16)
        first = once(("acc", i))
        for acc, val in ((acc_x, dot(xrows, wgu[j], NT)), (acc_d, dot(grows, wd[j], NT))):
            if first:
                acc[i] = val
            else:
                acc[i] += val

    def middle(i):
        rows = pl.ds(i * ROWS, ROWS)
        probe_i = acc_d[i][:, UNITS:].astype(BF16)
        probe[rows, :] = probe_i
        gate, up = acc_x[i][:, :UNITS], acc_x[i][:, UNITS:]
        dh = acc_d[i][:, :UNITS] + SCALE * dot(probe_i, lead[0])
        sig = jax.nn.sigmoid(gate)
        act = gate * sig
        hidden = (act * up).astype(BF16)
        hid[rows, :] = hidden
        dgate = dh * up * sig * (1.0 + gate * (1.0 - sig))
        dboth[i] = jnp.concatenate([dgate, dh * act], axis=1).astype(BF16)
        low_mine[:, i * ROWS : (i + 1) * ROWS] = dot(lead[0], hidden, NT)

    def sum_send(i, m, val):
        rows = SUMS[m][2]
        sum_out[i, m, 0:rows] = val.astype(BF16)
        send(
            sum_out.at[i, m, pl.ds(0, rows)], sum_in.at[i, m, pl.ds(0, rows)],
            rs_s.at[i, m], rs_r.at[i, m], way[SUMS[m][3]],
        )

    def sum_got(i, m):
        rows = SUMS[m][2]
        arrive(sum_in.at[i, m, pl.ds(0, rows)], rs_s.at[i, m], rs_r.at[i, m])
        return sum_in[i, m, 0:rows].astype(F32)

    def make(i, name):
        val = dot(dboth[i], wgu[ch[name]])
        part_sum[i, NAMES.index(name)] = val
        for m in MAKE[name]:
            sum_send(i, m, val[SUMS[m][1] : SUMS[m][1] + SUMS[m][2]])

    def add_to(val, base, i, m):
        at, n = SUMS[m][1] - base, SUMS[m][2]
        pieces = [val[:at], val[at : at + n] + sum_got(i, m), val[at + n :]]
        return jnp.concatenate([p for p in pieces if p.shape[0]], axis=0)

    def add_step(i, step):
        needs, m = ADDS[step]
        name, at, n, _ = SUMS[m]
        val = part_sum[i, NAMES.index(name), at : at + n]
        for k in needs:
            val = add_to(val, at, i, k)
        sum_send(i, m, val)

    def finish(i):
        val = part_sum[i, NAMES.index("o")]
        for m in LAST:
            val = add_to(val, 0, i, m)
        val = val.reshape(GPART, CSRC, WIDTH)
        ret_out[pl.ds(i * GPART, GPART)] = jnp.concatenate(
            [val[:, :, :512], val[:, :, 384:]], axis=1
        ).astype(BF16)
        for p in range(max(1, i * GPART), (i + 1) * GPART):
            send(ret_out.at[p], ret_in.at[p], ret_s.at[p], ret_r.at[p], expert_at(p, -1))

    for i, step in ORDER:
        if step in STEPS:
            gather_step(i, step)
        elif step in ADDS:
            add_step(i, step)
        elif step == "mid":
            middle(i)
            if i == PARTS - 1:
                for k, peer in enumerate(peers):
                    send(low_mine, low_all.at[k], low_s.at[k], low_r.at[k], peer)
        elif step == "end":
            finish(i)
        elif step[0] == "c":
            products(i, step[1:])
        else:
            make(i, step[1:])

    lead_out[0] = SCALE * dot(probe[...], hid[...], TN)
    grows = held[t].astype(F32)[:, CSRC:].reshape(GROUPS * CSRC, WIDTH).astype(BF16)
    low = low_mine[...]
    for k in range(TWIDE - 1):
        arrive(low_all.at[k], low_s.at[k], low_r.at[k])
        low = low + low_all[k]
    trail_out[0] = SCALE * dot(low.astype(BF16), grows)

    for p in range(1, GROUPS):
        arrive(ret_in.at[p], ret_s.at[p], ret_r.at[p])
    ret_in[0] = ret_out[0]
    back = ret_in[...].astype(F32)
    first = back[:, :CSRC].reshape(GROUPS * CSRC, 512).astype(BF16)
    last = back[:, CSRC:].reshape(GROUPS * CSRC, 512).astype(BF16)
    out[:, 0:512] = dot(pick[...], first, TN).astype(BF16)
    out[:, 512:WIDTH] = dot(pick[...], last, TN)[:, 128:].astype(BF16)

    for cp in started:
        cp.wait_send()


def on_device(tok, grad, routes, weights, wg, wu, wd, lead, trail):
    vm = pl.BlockSpec(memory_space=pltpu.VMEM)
    hbm = pl.BlockSpec(memory_space=pl.ANY)
    dma = pltpu.SemaphoreType.DMA
    dx, lead_t, trail_t = pl.pallas_call(
        kernel,
        out_shape=(
            jax.ShapeDtypeStruct((64, WIDTH), BF16),
            jax.ShapeDtypeStruct((1, RANK, UNITS), F32),
            jax.ShapeDtypeStruct((1, 16, WIDTH), F32),
        ),
        in_specs=[vm, vm, vm, vm, hbm, hbm, hbm, vm, vm],
        out_specs=(vm, vm, vm),
        scratch_shapes=[
            pltpu.VMEM((TWIDE, 2 * UNITS, WIDTH), BF16),
            pltpu.VMEM((TWIDE, UNITS + RANK, WIDTH), BF16),
            pltpu.VMEM((TWIDE, GROUPS, 16, WIDTH), BF16),
            pltpu.VMEM((GROUPS, 16, WIDTH), BF16),
            pltpu.VMEM((PARTS, ROWS, 2 * UNITS), F32),
            pltpu.VMEM((PARTS, ROWS, UNITS + RANK), F32),
            pltpu.VMEM((GROUPS * CSRC, UNITS), BF16),
            pltpu.VMEM((PARTS, ROWS, 2 * UNITS), BF16),
            pltpu.VMEM((GROUPS * CSRC, RANK), BF16),
            pltpu.VMEM((RANK, GROUPS * CSRC), F32),
            pltpu.VMEM((TWIDE - 1, RANK, GROUPS * CSRC), F32),
            pltpu.VMEM((PARTS, TWIDE, ROWS, WIDTH), F32),
            pltpu.VMEM((PARTS, len(SUMS), 32, WIDTH), BF16),
            pltpu.VMEM((PARTS, len(SUMS), 32, WIDTH), BF16),
            pltpu.VMEM((GROUPS, 16, 512), BF16),
            pltpu.VMEM((GROUPS, 16, 512), BF16),
            pltpu.VMEM((GROUPS * CSRC, 64), BF16),
            dma((3, TWIDE)),
            dma((GROUPS,)),
            dma((GROUPS,)),
            dma((TWIDE - 1,)),
            dma((TWIDE - 1,)),
            dma((PARTS, len(GATHER))),
            dma((PARTS, len(GATHER))),
            dma((PARTS, len(SUMS))),
            dma((PARTS, len(SUMS))),
            dma((TWIDE - 1,)),
            dma((TWIDE - 1,)),
            dma((GROUPS,)),
            dma((GROUPS,)),
            dma((2,)),
        ],
        compiler_params=pltpu.CompilerParams(
            collective_id=0, has_side_effects=True, vmem_limit_bytes=56 * 1024 * 1024
        ),
        cost_estimate=pl.CostEstimate(
            flops=6_000_000_000, bytes_accessed=16_000_000, transcendentals=80_000
        ),
    )(
        tok, grad, routes.T, weights.T, jnp.swapaxes(wg, 1, 2), jnp.swapaxes(wu, 1, 2),
        wd, jnp.swapaxes(lead, 1, 2), trail,
    )
    return dx, jnp.swapaxes(lead_t, 1, 2), trail_t


def solution(mesh):
    placed = (
        P("expert", "tensor"),
        P("expert", "tensor"),
        P("expert", None),
        P("expert", None),
        P("expert", None, "tensor"),
        P("expert", None, "tensor"),
        P("expert", "tensor", None),
        P("expert", "tensor", None),
        P("expert", None, "tensor"),
    )
    return jax.shard_map(
        on_device,
        mesh=mesh,
        in_specs=placed,
        out_specs=(P("expert", "tensor"), P("expert", "tensor", None), P("expert", None, "tensor")),
        check_vma=False,
    )
```

```python
import functools

import jax
import jax.numpy as jnp
from jax import lax
from jax.experimental import pallas as pl
from jax.experimental.pallas import tpu as pltpu
from jax.sharding import PartitionSpec as P

MESH = pl.DeviceIdType.MESH
F32, BF16 = jnp.float32, jnp.bfloat16
NT = (((1,), (1,)), ((), ()))
TN = (((0,), (0,)), ((), ()))

CSRC = 8
GROUPS = 32
PARTS = 4
GPART = GROUPS // PARTS
ROWS = GPART * CSRC
WIDTH = 896
UNITS = 304
RANK = 16
TWIDE = 8
SCALE = 2.0


def pair(m, dc):
    return tuple((dz, dyl, dc) for dz in (m, 8 - m) for dyl in range(2))


PLACES = (
    tuple((0, p // 2, p % 2) for p in range(4))
    + sum((pair(m, dc) for m in (1, 2, 3) for dc in range(2)), ())
    + tuple((4, p // 2, p % 2) for p in range(4))
)

CUTS = ((3, 3, 1, 1), (3, 3, 1, 1), (3, 3, 1, 1), (3, 3, 1, 1))


def cut(i, key):
    b1, b2, a1, a2 = CUTS[i][2], CUTS[i][3], CUTS[i][0], CUTS[i][1]
    b = b1 + b2
    at, n = {
        "B1": (0, b1), "B2": (b1, b2), "B": (0, b), "A1": (b, a1), "A2": (b + a1, a2), "A": (b, a1 + a2),
    }[key]
    return i * GPART + at, n


GATHER = (
    ("o", "A", "y", "po"), ("o", "B", "r", "l"), ("o", "B", "l", "r"), ("o", "B", "y", "po"),
    ("o", "A", "r", "l"), ("o", "A", "l", "r"), ("l", "B1", "r", "2"), ("r", "B2", "l", "2"),
    ("l", "B", "y", "pl"), ("r", "B", "y", "pr"), ("2", "B1", "y", "p2"), ("2", "B2", "y", "p2"),
    ("l", "A1", "r", "2"), ("r", "A2", "l", "2"), ("po", "A", "r", "pl"), ("po", "A", "l", "pr"),
    ("pl", "A1", "r", "p2"), ("pr", "A2", "l", "p2"),
)
STEPS = {
    "g0": ((), (1, 2, 3)), "g1": ((), (0, 4, 5)), "g2": ((1,), (6, 8)), "g3": ((2,), (7, 9)),
    "g4": ((0,), (14, 15)), "g5": ((4,), (12,)), "g6": ((5,), (13,)), "g7": ((6,), (10,)),
    "g8": ((7,), (11,)), "g9": ((14,), (16,)), "g10": ((15,), (17,)),
}
CHUNKS = {
    "o": (), "l": (1, 4), "r": (2, 5), "2": (6, 7, 12, 13), "po": (0, 3), "pl": (14, 8), "pr": (15, 9),
    "p2": (16, 17, 10, 11),
}
SUMS = (
    ("p2", 0, 16, "r"), ("p2", 16, 16, "l"), ("p2", 32, 32, "y"), ("pr", 32, 32, "y"), ("pl", 32, 32, "y"),
    ("po", 32, 32, "y"), ("pr", 0, 32, "r"), ("pl", 0, 32, "l"), ("po", 0, 32, "y"), ("2", 0, 32, "r"),
    ("2", 32, 32, "l"), ("r", 0, 32, "r"), ("l", 0, 32, "l"), ("r", 32, 32, "r"), ("l", 32, 32, "l"),
)
MAKE = {"p2": (0, 1, 2), "pr": (3,), "pl": (4,), "po": (5,), "2": (9,), "l": (12,), "r": (), "o": ()}
ADDS = {
    "s0": ((0,), 6), "s1": ((1,), 7), "s2": ((6, 7), 8), "s3": ((2,), 10), "s4": ((9,), 11), "s5": ((3,), 13),
    "s6": ((10, 4), 14),
}
LAST = (5, 8, 11, 12, 13, 14)

NAMES = tuple(CHUNKS)

ORDER = (
    (0, "g0"), (0, "g1"), (0, "co"), (1, "g0"), (1, "g1"), (1, "co"), (0, "g2"), (0, "g3"), (0, "g4"),
    (0, "g5"), (0, "g6"), (0, "cl"), (0, "cr"), (1, "g2"), (1, "g3"), (0, "cpo"), (1, "g4"), (1, "g5"),
    (1, "g6"), (1, "cpo"), (0, "g7"), (0, "g8"), (2, "g0"), (2, "g1"), (1, "cr"), (1, "cl"), (2, "co"),
    (0, "g9"), (0, "g10"), (0, "cpr"), (0, "cpl"), (0, "c2"), (1, "g7"), (1, "g8"), (3, "g0"), (3, "g1"),
    (3, "co"), (1, "g9"), (1, "g10"), (1, "cpl"), (2, "g4"), (1, "cpr"), (2, "cpo"), (1, "c2"), (2, "g2"),
    (2, "g3"), (2, "g5"), (2, "g6"), (3, "g4"), (2, "cl"), (2, "cr"), (3, "cpo"), (0, "cp2"), (0, "mid"),
    (0, "dp2"), (3, "g2"), (3, "g3"), (0, "dpr"), (0, "dpl"), (0, "dpo"), (0, "d2"), (0, "dr"), (0, "dl"),
    (0, "do"), (0, "s3"), (3, "g5"), (3, "g6"), (3, "cr"), (3, "cl"), (1, "cp2"), (1, "mid"), (0, "s5"),
    (1, "dp2"), (1, "dpr"), (1, "dpl"), (1, "dpo"), (1, "d2"), (1, "dr"), (1, "dl"), (1, "do"), (2, "g9"),
    (2, "g10"), (2, "cpr"), (2, "g7"), (2, "g8"), (1, "s3"), (2, "cpl"), (1, "s5"), (2, "c2"), (3, "g9"),
    (3, "g10"), (3, "cpr"), (0, "s0"), (0, "s1"), (3, "g7"), (3, "g8"), (3, "cpl"), (0, "s4"), (0, "s6"),
    (3, "c2"), (1, "s0"), (1, "s1"), (1, "s4"), (2, "cp2"), (2, "mid"), (2, "dp2"), (2, "dpr"), (1, "s6"),
    (2, "dpl"), (2, "dpo"), (2, "d2"), (2, "dr"), (2, "dl"), (2, "do"), (3, "cp2"), (2, "s3"), (0, "s2"),
    (3, "mid"), (3, "dp2"), (2, "s5"), (3, "dpr"), (3, "dpl"), (3, "dpo"), (3, "d2"), (3, "dr"), (1, "s2"),
    (3, "dl"), (2, "s1"), (3, "do"), (2, "s0"), (0, "end"), (2, "s4"), (3, "s3"), (3, "s0"), (2, "s6"),
    (3, "s5"), (3, "s1"), (3, "s4"), (2, "s2"), (1, "end"), (3, "s6"), (2, "end"), (3, "s2"), (3, "end"),
)


def dot(a, b, dims=(((1,), (0,)), ((), ()))):
    return lax.dot_general(a, b, dims, preferred_element_type=F32)


def kernel(
    tok_in, grad_in, routes_in, weights_in, wg_hbm, wu_hbm, wd_hbm, lead_in, trail_in,
    out, lead_out, trail_out,
    wgu, wd, held, sendbuf, acc_x, acc_d, hid, dboth, probe, low_mine, low_all, part_sum,
    sum_out, sum_in, ret_out, ret_in, pick, tok, grad, routes, weights, lead, trail, mixed,
    w_sem, a2a_s, a2a_r, b_s, b_r, ag_s, ag_r, rs_s, rs_r, low_s, low_r, ret_s, ret_r, loc_sem, in_sem,
):
    e = lax.axis_index("expert")
    t = lax.axis_index("tensor")
    z, yl, c = e // 4, (e // 2) % 2, e % 2
    yh, x = t // 4, t % 4
    xr, xl, x2, yo = (x + 1) % 4, (x + 3) % 4, (x + 2) % 4, 1 - yh
    way = {"r": (e, yh * 4 + xr), "l": (e, yh * 4 + xl), "y": (e, yo * 4 + x)}
    col = {"o": x, "r": xr, "l": xl, "2": x2}
    ch = {k: yh * 4 + v for k, v in col.items()}
    ch.update({"p" + k: yo * 4 + v for k, v in col.items()})

    def expert_at(p, sign):
        dz, dyl, dc = PLACES[p]
        zz = (z + (dz if sign > 0 else 8 - dz)) % 8
        yy = 1 - yl if dyl else yl
        cc = 1 - c if dc else c
        return (zz * 4 + yy * 2 + cc, t)

    peers = [(e, (t + k) % TWIDE) for k in range(1, TWIDE)]

    small = [
        pltpu.make_async_copy(src, dst, in_sem.at[k])
        for k, (src, dst) in enumerate(
            ((routes_in, routes), (weights_in, weights), (tok_in, tok), (grad_in, grad), (lead_in, lead), (trail_in, trail))
        )
    ]
    for cp in small:
        cp.start()

    w_copies = []
    for j in range(TWIDE):
        cols = pl.ds(j * WIDTH, WIDTH)
        for i, (src, dst, at) in enumerate(((wg_hbm, wgu, 0), (wu_hbm, wgu, UNITS), (wd_hbm, wd, 0))):
            w_copies.append(
                pltpu.make_async_copy(
                    src.at[0, :, cols], dst.at[j, pl.ds(at, UNITS)], w_sem.at[i, j]
                )
            )
    w_copies.append(
        pltpu.make_async_copy(trail_in.at[0], wd.at[t, pl.ds(UNITS, RANK)], loc_sem.at[1])
    )

    barrier = pltpu.get_barrier_semaphore()
    for p in range(1, GROUPS):
        pl.semaphore_signal(barrier, inc=1, device_id=expert_at(p, 1), device_id_type=MESH)
    for peer in peers:
        pl.semaphore_signal(barrier, inc=1, device_id=peer, device_id_type=MESH)
    for cp in w_copies:
        cp.start()

    for cp in small:
        cp.wait()
    experts = lax.broadcasted_iota(jnp.int32, (GROUPS, 64), 0)
    hot = [(routes[k : k + 1, :] == experts).astype(F32) for k in range(2)]
    upper = (
        lax.broadcasted_iota(jnp.int32, (64, 64), 0) < lax.broadcasted_iota(jnp.int32, (64, 64), 1)
    ).astype(BF16)
    earlier = dot((hot[0] + hot[1]).astype(BF16), upper)
    slots = lax.broadcasted_iota(jnp.int32, (GROUPS * CSRC, 64), 0)
    picks = []
    for k in range(2):
        rk = routes[k : k + 1, :]
        dz = ((rk >> 2) - z) & 7
        dyl, dc = ((rk >> 1) & 1) ^ yl, (rk & 1) ^ c
        m = jnp.minimum(dz, 8 - dz)
        place = jnp.where(
            m % 4 == 0,
            m * 7 + dyl * 2 + dc,
            m * 8 - 4 + dc * 4 + jnp.where(dz > 4, 2, 0) + dyl,
        )
        slot = jnp.sum(earlier * hot[k], axis=0, keepdims=True).astype(jnp.int32)
        picks.append(((place * CSRC + slot) == slots).astype(F32))
    both = (picks[0] + picks[1]).astype(BF16)
    pick[...] = both
    xs = dot(both, tok[...])
    factor = picks[0] * weights[0:1, :] + picks[1] * weights[1:2, :]
    gs = jnp.sum(factor, axis=1, keepdims=True) * dot(both, grad[...])
    packed = jnp.concatenate(
        [xs.reshape(GROUPS, CSRC, WIDTH), gs.reshape(GROUPS, CSRC, WIDTH)], axis=1
    ).astype(BF16)
    sendbuf[...] = packed

    pl.semaphore_wait(barrier, GROUPS - 1 + len(peers))

    started = []

    def remote(src, dst, ss, rs, dev):
        return pltpu.make_async_remote_copy(
            src_ref=src, dst_ref=dst, send_sem=ss, recv_sem=rs, device_id=dev, device_id_type=MESH
        )

    def send(*args):
        cp = remote(*args)
        cp.start()
        started.append(cp)

    def arrive(dst, ss, rs):
        remote(dst, dst, ss, rs, way["y"]).wait_recv()

    def exchange(groups):
        for p in groups:
            send(sendbuf.at[p], held.at[t, p], a2a_s.at[p], a2a_r.at[p], expert_at(p, 1))

    own_copy = pltpu.make_async_copy(sendbuf.at[0], held.at[t, 0], loc_sem.at[0])
    own_copy.start()
    exchange(range(1, GPART))

    done = set()

    def once(key):
        new = key not in done
        done.add(key)
        return new

    def have_own(i, key):
        at, n = cut(i, key)
        for p in range(at, at + n):
            if p and once(("own", p)):
                arrive(held.at[t, p], a2a_s.at[p], a2a_r.at[p])
        if i == 0 and once("copied"):
            own_copy.wait()

    def region(name, i, key):
        at, n = cut(i, key)
        return held.at[ch[name], pl.ds(at, n)]

    def gather_step(i, step):
        needs, sends = STEPS[step]
        if step in ("g0", "g1"):
            have_own(i, "B" if step == "g0" else "A")
        gathered(i, needs)
        for m in sends:
            name, key, to, _ = GATHER[m]
            ref = region(name, i, key)
            send(ref, ref, ag_s.at[i, m], ag_r.at[i, m], way[to])
        if step == "g1" and i < 2:
            exchange(range(GPART, 2 * GPART) if i == 0 else range(2 * GPART, GROUPS))
        if step == "g1" and i == 0:
            for k, peer in enumerate(peers):
                send(trail.at[0], wd.at[t, pl.ds(UNITS, RANK)], b_s.at[k], b_r.at[k], peer)

    def gathered(i, needs):
        for m in needs:
            if once(("g", i, m)):
                arrive(region(GATHER[m][3], i, GATHER[m][1]), ag_s.at[i, m], ag_r.at[i, m])

    def products(i, name):
        gathered(i, CHUNKS[name])
        if once("weights"):
            for cp in w_copies:
                cp.wait()
        if name != "o" and once("adapter"):
            for k in range(TWIDE - 1):
                arrive(wd.at[(t + TWIDE - 1 - k) % TWIDE, pl.ds(UNITS, RANK)], b_s.at[k], b_r.at[k])
        j = ch[name]
        block = held[j, pl.ds(i * GPART, GPART)].astype(F32)
        xrows = block[:, :CSRC].reshape(ROWS, WIDTH).astype(BF16)
        grows = block[:, CSRC:].reshape(ROWS, WIDTH).astype(BF16)
        first = once(("acc", i))
        for acc, val in ((acc_x, dot(xrows, wgu[j], NT)), (acc_d, dot(grows, wd[j], NT))):
            if first:
                acc[i] = val
            else:
                acc[i] += val

    def middle(i):
        rows = pl.ds(i * ROWS, ROWS)
        probe_i = acc_d[i][:, UNITS:].astype(BF16)
        probe[rows, :] = probe_i
        gate, up = acc_x[i][:, :UNITS], acc_x[i][:, UNITS:]
        dh = acc_d[i][:, :UNITS] + SCALE * dot(probe_i, lead[0])
        sig = jax.nn.sigmoid(gate)
        act = gate * sig
        hidden = (act * up).astype(BF16)
        hid[rows, :] = hidden
        dgate = dh * up * sig * (1.0 + gate * (1.0 - sig))
        dboth[i] = jnp.concatenate([dgate, dh * act], axis=1).astype(BF16)
        low_mine[:, i * ROWS : (i + 1) * ROWS] = dot(lead[0], hidden, NT)

    def sum_send(i, m, val):
        rows = SUMS[m][2]
        sum_out[i, m, 0:rows] = val.astype(BF16)
        send(
            sum_out.at[i, m, pl.ds(0, rows)], sum_in.at[i, m, pl.ds(0, rows)],
            rs_s.at[i, m], rs_r.at[i, m], way[SUMS[m][3]],
        )

    def sum_got(i, m):
        rows = SUMS[m][2]
        arrive(sum_in.at[i, m, pl.ds(0, rows)], rs_s.at[i, m], rs_r.at[i, m])
        return sum_in[i, m, 0:rows].astype(F32)

    def make(i, name):
        val = dot(dboth[i], wgu[ch[name]])
        part_sum[i, NAMES.index(name)] = val
        for m in MAKE[name]:
            sum_send(i, m, val[SUMS[m][1] : SUMS[m][1] + SUMS[m][2]])

    def add_to(val, base, i, m):
        at, n = SUMS[m][1] - base, SUMS[m][2]
        pieces = [val[:at], val[at : at + n] + sum_got(i, m), val[at + n :]]
        return jnp.concatenate([p for p in pieces if p.shape[0]], axis=0)

    def add_step(i, step):
        needs, m = ADDS[step]
        name, at, n, _ = SUMS[m]
        val = part_sum[i, NAMES.index(name), at : at + n]
        for k in needs:
            val = add_to(val, at, i, k)
        sum_send(i, m, val)

    def finish(i):
        val = part_sum[i, NAMES.index("o")]
        for m in LAST:
            val = add_to(val, 0, i, m)
        val = val.reshape(GPART, CSRC, WIDTH)
        ret_out[pl.ds(i * GPART, GPART)] = jnp.concatenate(
            [val[:, :, :512], val[:, :, 384:]], axis=1
        ).astype(BF16)
        for p in range(max(1, i * GPART), (i + 1) * GPART):
            send(ret_out.at[p], ret_in.at[p], ret_s.at[p], ret_r.at[p], expert_at(p, -1))

    def combine(i):
        for p in range(max(1, i * GPART), (i + 1) * GPART):
            arrive(ret_in.at[p], ret_s.at[p], ret_r.at[p])
        if i == 0:
            ret_in[0] = ret_out[0]
        back = ret_in[pl.ds(i * GPART, GPART)].astype(F32)
        first = back[:, :CSRC].reshape(ROWS, 512).astype(BF16)
        last = back[:, CSRC:, 128:].reshape(ROWS, WIDTH - 512).astype(BF16)
        rows = pick[pl.ds(i * ROWS, ROWS), :]
        return jnp.concatenate([dot(rows, first, TN), dot(rows, last, TN)], axis=1)

    def adapters():
        lead_out[0] = SCALE * dot(probe[...], hid[...], TN)
        grows = held[t].astype(F32)[:, CSRC:].reshape(GROUPS * CSRC, WIDTH).astype(BF16)
        low = low_mine[...]
        for k in range(TWIDE - 1):
            arrive(low_all.at[k], low_s.at[k], low_r.at[k])
            low = low + low_all[k]
        trail_out[0] = SCALE * dot(low.astype(BF16), grows)

    for i, step in ORDER:
        if step in STEPS:
            gather_step(i, step)
        elif step in ADDS:
            add_step(i, step)
        elif step == "mid":
            middle(i)
            if i == PARTS - 1:
                for k, peer in enumerate(peers):
                    send(low_mine, low_all.at[k], low_s.at[k], low_r.at[k], peer)
        elif step == "end":
            if i == PARTS - 1:
                adapters()
                mixed[...] = combine(0)
            finish(i)
        elif step[0] == "c":
            products(i, step[1:])
        else:
            make(i, step[1:])

    total = mixed[...]
    for i in range(1, PARTS):
        total = total + combine(i)
    out[...] = total.astype(BF16)

    for cp in started:
        cp.wait_send()


def copy_out(a, b, c, x, y, z):
    x[...] = a[...]
    y[...] = b[...]
    z[...] = c[...]


def on_device(tok, grad, routes, weights, wg, wu, wd, lead, trail):
    vm = pl.BlockSpec(memory_space=pltpu.VMEM)
    hbm = pl.BlockSpec(memory_space=pl.ANY)
    dma = pltpu.SemaphoreType.DMA
    dx, lead_t, trail_t = pl.pallas_call(
        kernel,
        out_shape=(
            jax.ShapeDtypeStruct((64, WIDTH), BF16),
            jax.ShapeDtypeStruct((1, RANK, UNITS), F32),
            jax.ShapeDtypeStruct((1, 16, WIDTH), F32),
        ),
        in_specs=[hbm] * 9,
        out_specs=(vm, vm, vm),
        scratch_shapes=[
            pltpu.VMEM((TWIDE, 2 * UNITS, WIDTH), BF16),
            pltpu.VMEM((TWIDE, UNITS + RANK, WIDTH), BF16),
            pltpu.VMEM((TWIDE, GROUPS, 16, WIDTH), BF16),
            pltpu.VMEM((GROUPS, 16, WIDTH), BF16),
            pltpu.VMEM((PARTS, ROWS, 2 * UNITS), F32),
            pltpu.VMEM((PARTS, ROWS, UNITS + RANK), F32),
            pltpu.VMEM((GROUPS * CSRC, UNITS), BF16),
            pltpu.VMEM((PARTS, ROWS, 2 * UNITS), BF16),
            pltpu.VMEM((GROUPS * CSRC, RANK), BF16),
            pltpu.VMEM((RANK, GROUPS * CSRC), F32),
            pltpu.VMEM((TWIDE - 1, RANK, GROUPS * CSRC), F32),
            pltpu.VMEM((PARTS, TWIDE, ROWS, WIDTH), F32),
            pltpu.VMEM((PARTS, len(SUMS), 32, WIDTH), BF16),
            pltpu.VMEM((PARTS, len(SUMS), 32, WIDTH), BF16),
            pltpu.VMEM((GROUPS, 16, 512), BF16),
            pltpu.VMEM((GROUPS, 16, 512), BF16),
            pltpu.VMEM((GROUPS * CSRC, 64), BF16),
            pltpu.VMEM((64, WIDTH), BF16),
            pltpu.VMEM((64, WIDTH), BF16),
            pltpu.VMEM((2, 64), jnp.int32),
            pltpu.VMEM((2, 64), F32),
            pltpu.VMEM((1, RANK, UNITS), BF16),
            pltpu.VMEM((1, RANK, WIDTH), BF16),
            pltpu.VMEM((64, WIDTH), F32),
            dma((3, TWIDE)),
            dma((GROUPS,)),
            dma((GROUPS,)),
            dma((TWIDE - 1,)),
            dma((TWIDE - 1,)),
            dma((PARTS, len(GATHER))),
            dma((PARTS, len(GATHER))),
            dma((PARTS, len(SUMS))),
            dma((PARTS, len(SUMS))),
            dma((TWIDE - 1,)),
            dma((TWIDE - 1,)),
            dma((GROUPS,)),
            dma((GROUPS,)),
            dma((2,)),
            dma((6,)),
        ],
        compiler_params=pltpu.CompilerParams(
            collective_id=0, has_side_effects=True, vmem_limit_bytes=56 * 1024 * 1024
        ),
        cost_estimate=pl.CostEstimate(
            flops=6_000_000_000, bytes_accessed=16_000_000, transcendentals=80_000
        ),
    )(
        tok, grad, routes.T, weights.T, jnp.swapaxes(wg, 1, 2), jnp.swapaxes(wu, 1, 2),
        wd, jnp.swapaxes(lead, 1, 2), trail,
    )
    results = (dx, lead_t, trail_t)
    dx, lead_t, trail_t = pl.pallas_call(
        copy_out,
        out_shape=tuple(jax.ShapeDtypeStruct(v.shape, v.dtype) for v in results),
        in_specs=[vm] * 3,
        out_specs=(vm,) * 3,
    )(*results)
    return dx, jnp.swapaxes(lead_t, 1, 2), trail_t


def solution(mesh):
    placed = (
        P("expert", "tensor"),
        P("expert", "tensor"),
        P("expert", None),
        P("expert", None),
        P("expert", None, "tensor"),
        P("expert", None, "tensor"),
        P("expert", "tensor", None),
        P("expert", "tensor", None),
        P("expert", None, "tensor"),
    )
    return jax.shard_map(
        on_device,
        mesh=mesh,
        in_specs=placed,
        out_specs=(P("expert", "tensor"), P("expert", "tensor", None), P("expert", None, "tensor")),
        check_vma=False,
    )
```

```python
import functools

import jax
import jax.numpy as jnp
from jax import lax
from jax.experimental import pallas as pl
from jax.experimental.pallas import tpu as pltpu
from jax.sharding import PartitionSpec as P

MESH = pl.DeviceIdType.MESH
F32, BF16 = jnp.float32, jnp.bfloat16
NT = (((1,), (1,)), ((), ()))
TN = (((0,), (0,)), ((), ()))

CSRC = 8
GROUPS = 32
PARTS = 4
GPART = GROUPS // PARTS
ROWS = GPART * CSRC
WIDTH = 896
UNITS = 304
RANK = 16
TWIDE = 8
SCALE = 2.0


def pair(m, dc):
    return tuple((dz, dyl, dc) for dz in (m, 8 - m) for dyl in range(2))


PLACES = (
    tuple((0, p // 2, p % 2) for p in range(4))
    + sum((pair(m, dc) for m in (1, 2, 3) for dc in range(2)), ())
    + tuple((4, p // 2, p % 2) for p in range(4))
)

CUTS = ((3, 3, 1, 1), (3, 3, 1, 1), (3, 3, 1, 1), (3, 3, 1, 1))


def cut(i, key):
    b1, b2, a1, a2 = CUTS[i][2], CUTS[i][3], CUTS[i][0], CUTS[i][1]
    b = b1 + b2
    at, n = {
        "B1": (0, b1), "B2": (b1, b2), "B": (0, b), "A1": (b, a1), "A2": (b + a1, a2), "A": (b, a1 + a2),
    }[key]
    return i * GPART + at, n


GATHER = (
    ("o", "A", "y", "po"), ("o", "B", "r", "l"), ("o", "B", "l", "r"), ("o", "B", "y", "po"),
    ("o", "A", "r", "l"), ("o", "A", "l", "r"), ("l", "B1", "r", "2"), ("r", "B2", "l", "2"),
    ("l", "B", "y", "pl"), ("r", "B", "y", "pr"), ("2", "B1", "y", "p2"), ("2", "B2", "y", "p2"),
    ("l", "A1", "r", "2"), ("r", "A2", "l", "2"), ("po", "A", "r", "pl"), ("po", "A", "l", "pr"),
    ("pl", "A1", "r", "p2"), ("pr", "A2", "l", "p2"),
)
STEPS = {
    "g0": ((), (1, 2, 3)), "g1": ((), (0, 4, 5)), "g2": ((1,), (6, 8)), "g3": ((2,), (7, 9)),
    "g4": ((0,), (14, 15)), "g5": ((4,), (12,)), "g6": ((5,), (13,)), "g7": ((6,), (10,)),
    "g8": ((7,), (11,)), "g9": ((14,), (16,)), "g10": ((15,), (17,)),
}
CHUNKS = {
    "o": (), "l": (1, 4), "r": (2, 5), "2": (6, 7, 12, 13), "po": (0, 3), "pl": (14, 8), "pr": (15, 9),
    "p2": (16, 17, 10, 11),
}
SUMS = (
    ("p2", 0, 16, "r"), ("p2", 16, 16, "l"), ("p2", 32, 32, "y"), ("pr", 32, 32, "y"), ("pl", 32, 32, "y"),
    ("po", 32, 32, "y"), ("pr", 0, 32, "r"), ("pl", 0, 32, "l"), ("po", 0, 32, "y"), ("2", 0, 32, "r"),
    ("2", 32, 32, "l"), ("r", 0, 32, "r"), ("l", 0, 32, "l"), ("r", 32, 32, "r"), ("l", 32, 32, "l"),
)
MAKE = {"p2": (0, 1, 2), "pr": (3,), "pl": (4,), "po": (5,), "2": (9,), "l": (12,), "r": (), "o": ()}
ADDS = {
    "s0": ((0,), 6), "s1": ((1,), 7), "s2": ((6, 7), 8), "s3": ((2,), 10), "s4": ((9,), 11), "s5": ((3,), 13),
    "s6": ((10, 4), 14),
}
LAST = (5, 8, 11, 12, 13, 14)

NAMES = tuple(CHUNKS)

ORDER = (
    (0, "g0"), (0, "g1"), (0, "co"), (0, "g2"), (0, "g3"), (1, "g0"), (1, "g1"), (1, "co"), (0, "g4"),
    (0, "g5"), (0, "g6"), (0, "cpo"), (0, "g7"), (0, "g8"), (0, "cl"), (1, "g2"), (1, "g3"), (2, "g0"),
    (2, "g1"), (0, "cr"), (2, "co"), (1, "g5"), (1, "g6"), (1, "cr"), (1, "cl"), (1, "g4"), (3, "g0"),
    (3, "g1"), (1, "cpo"), (3, "co"), (0, "g9"), (0, "g10"), (0, "cpl"), (0, "c2"), (1, "g7"), (1, "g8"),
    (0, "cpr"), (2, "g2"), (2, "g3"), (2, "g4"), (2, "cpo"), (2, "g5"), (2, "g6"), (2, "cr"), (2, "cl"),
    (1, "c2"), (3, "g4"), (3, "cpo"), (1, "g9"), (1, "g10"), (1, "cpr"), (1, "cpl"), (3, "g2"), (3, "g3"),
    (3, "g5"), (3, "g6"), (3, "cr"), (3, "cl"), (0, "cp2"), (2, "g7"), (2, "g8"), (0, "mid"), (0, "dp2"),
    (0, "dpr"), (0, "dpl"), (0, "dpo"), (0, "d2"), (0, "dr"), (0, "s3"), (2, "g9"), (2, "g10"), (0, "dl"),
    (0, "do"), (0, "s5"), (2, "cpl"), (2, "c2"), (2, "cpr"), (3, "g9"), (3, "g10"), (3, "cpr"), (3, "cpl"),
    (1, "cp2"), (3, "g7"), (3, "g8"), (1, "mid"), (1, "dp2"), (1, "dpr"), (1, "dpl"), (0, "s0"), (0, "s1"),
    (1, "dpo"), (0, "s6"), (0, "s4"), (1, "d2"), (1, "s3"), (1, "dr"), (1, "s5"), (1, "dl"), (1, "do"),
    (2, "cp2"), (2, "mid"), (2, "dp2"), (2, "dpr"), (2, "dpl"), (1, "s0"), (1, "s1"), (2, "dpo"), (0, "s2"),
    (2, "d2"), (2, "s3"), (2, "dr"), (2, "s5"), (2, "dl"), (1, "s6"), (1, "s4"), (2, "do"), (3, "c2"),
    (2, "s0"), (2, "s1"), (3, "cp2"), (0, "end"), (1, "s2"), (2, "s4"), (2, "s6"), (3, "mid"), (3, "dp2"),
    (3, "dpr"), (3, "dpl"), (1, "end"), (3, "dpo"), (2, "s2"), (3, "d2"), (3, "s3"), (3, "dr"), (3, "s0"),
    (3, "s5"), (3, "s1"), (3, "dl"), (3, "s4"), (3, "s6"), (3, "do"), (3, "s2"), (2, "end"), (3, "end"),
)


def dot(a, b, dims=(((1,), (0,)), ((), ()))):
    return lax.dot_general(a, b, dims, preferred_element_type=F32)


def kernel(
    tok_in, grad_in, routes_in, weights_in, wg_hbm, wu_hbm, wd_hbm, lead_in, trail_in,
    out, lead_out, trail_out,
    wgu, wd, held, sendbuf, acc_x, acc_d, hid, dboth, probe, low_mine, low_all, part_sum,
    sum_out, sum_in, ret_out, ret_in, pick, tok, grad, routes, weights, lead, trail, mixed,
    w_sem, a2a_s, a2a_r, b_s, b_r, ag_s, ag_r, rs_s, rs_r, low_s, low_r, ret_s, ret_r, loc_sem, in_sem,
):
    e = lax.axis_index("expert")
    t = lax.axis_index("tensor")
    z, yl, c = e // 4, (e // 2) % 2, e % 2
    yh, x = t // 4, t % 4
    xr, xl, x2, yo = (x + 1) % 4, (x + 3) % 4, (x + 2) % 4, 1 - yh
    way = {"r": (e, yh * 4 + xr), "l": (e, yh * 4 + xl), "y": (e, yo * 4 + x)}
    col = {"o": x, "r": xr, "l": xl, "2": x2}
    ch = {k: yh * 4 + v for k, v in col.items()}
    ch.update({"p" + k: yo * 4 + v for k, v in col.items()})

    def expert_at(p, sign):
        dz, dyl, dc = PLACES[p]
        zz = (z + (dz if sign > 0 else 8 - dz)) % 8
        yy = 1 - yl if dyl else yl
        cc = 1 - c if dc else c
        return (zz * 4 + yy * 2 + cc, t)

    peers = [(e, (t + k) % TWIDE) for k in range(1, TWIDE)]

    small = [
        pltpu.make_async_copy(src, dst, in_sem.at[k])
        for k, (src, dst) in enumerate(
            ((routes_in, routes), (weights_in, weights), (tok_in, tok), (grad_in, grad), (lead_in, lead), (trail_in, trail))
        )
    ]
    for cp in small:
        cp.start()

    w_copies = []
    for j in range(TWIDE):
        cols = pl.ds(j * WIDTH, WIDTH)
        for i, (src, dst, at) in enumerate(((wg_hbm, wgu, 0), (wu_hbm, wgu, UNITS), (wd_hbm, wd, 0))):
            w_copies.append(
                pltpu.make_async_copy(
                    src.at[0, :, cols], dst.at[j, pl.ds(at, UNITS)], w_sem.at[i, j]
                )
            )
    w_copies.append(
        pltpu.make_async_copy(trail_in.at[0], wd.at[t, pl.ds(UNITS, RANK)], loc_sem.at[1])
    )

    barrier = pltpu.get_barrier_semaphore()
    for p in range(1, GROUPS):
        pl.semaphore_signal(barrier, inc=1, device_id=expert_at(p, 1), device_id_type=MESH)
    for peer in peers:
        pl.semaphore_signal(barrier, inc=1, device_id=peer, device_id_type=MESH)
    for cp in w_copies:
        cp.start()

    for cp in small:
        cp.wait()
    experts = lax.broadcasted_iota(jnp.int32, (GROUPS, 64), 0)
    hot = [(routes[k : k + 1, :] == experts).astype(F32) for k in range(2)]
    upper = (
        lax.broadcasted_iota(jnp.int32, (64, 64), 0) < lax.broadcasted_iota(jnp.int32, (64, 64), 1)
    ).astype(BF16)
    earlier = dot((hot[0] + hot[1]).astype(BF16), upper)
    slots = lax.broadcasted_iota(jnp.int32, (GROUPS * CSRC, 64), 0)
    picks = []
    for k in range(2):
        rk = routes[k : k + 1, :]
        dz = ((rk >> 2) - z) & 7
        dyl, dc = ((rk >> 1) & 1) ^ yl, (rk & 1) ^ c
        m = jnp.minimum(dz, 8 - dz)
        place = jnp.where(
            m % 4 == 0,
            m * 7 + dyl * 2 + dc,
            m * 8 - 4 + dc * 4 + jnp.where(dz > 4, 2, 0) + dyl,
        )
        slot = jnp.sum(earlier * hot[k], axis=0, keepdims=True).astype(jnp.int32)
        picks.append(((place * CSRC + slot) == slots).astype(F32))
    both = (picks[0] + picks[1]).astype(BF16)
    pick[...] = both
    xs = dot(both, tok[...])
    factor = picks[0] * weights[0:1, :] + picks[1] * weights[1:2, :]
    gs = jnp.sum(factor, axis=1, keepdims=True) * dot(both, grad[...])
    packed = jnp.concatenate(
        [xs.reshape(GROUPS, CSRC, WIDTH), gs.reshape(GROUPS, CSRC, WIDTH)], axis=1
    ).astype(BF16)
    sendbuf[...] = packed

    pl.semaphore_wait(barrier, GROUPS - 1 + len(peers))

    started = []

    def remote(src, dst, ss, rs, dev):
        return pltpu.make_async_remote_copy(
            src_ref=src, dst_ref=dst, send_sem=ss, recv_sem=rs, device_id=dev, device_id_type=MESH
        )

    def send(*args):
        cp = remote(*args)
        cp.start()
        started.append(cp)

    def arrive(dst, ss, rs):
        remote(dst, dst, ss, rs, way["y"]).wait_recv()

    def exchange(groups):
        for p in groups:
            send(sendbuf.at[p], held.at[t, p], a2a_s.at[p], a2a_r.at[p], expert_at(p, 1))

    own_copy = pltpu.make_async_copy(sendbuf.at[0], held.at[t, 0], loc_sem.at[0])
    own_copy.start()
    exchange(range(1, GPART))

    done = set()

    def once(key):
        new = key not in done
        done.add(key)
        return new

    def have_own(i, key):
        at, n = cut(i, key)
        for p in range(at, at + n):
            if p and once(("own", p)):
                arrive(held.at[t, p], a2a_s.at[p], a2a_r.at[p])
        if i == 0 and once("copied"):
            own_copy.wait()

    def region(name, i, key):
        at, n = cut(i, key)
        return held.at[ch[name], pl.ds(at, n)]

    def gather_step(i, step):
        needs, sends = STEPS[step]
        if step in ("g0", "g1"):
            have_own(i, "B" if step == "g0" else "A")
        gathered(i, needs)
        for m in sends:
            name, key, to, _ = GATHER[m]
            ref = region(name, i, key)
            send(ref, ref, ag_s.at[i, m], ag_r.at[i, m], way[to])
        if step == "g1" and i < 2:
            exchange(range(GPART, 2 * GPART) if i == 0 else range(2 * GPART, GROUPS))
        if step == "g1" and i == 0:
            for k, peer in enumerate(peers):
                send(trail.at[0], wd.at[t, pl.ds(UNITS, RANK)], b_s.at[k], b_r.at[k], peer)

    def gathered(i, needs):
        for m in needs:
            if once(("g", i, m)):
                arrive(region(GATHER[m][3], i, GATHER[m][1]), ag_s.at[i, m], ag_r.at[i, m])

    def products(i, name):
        gathered(i, CHUNKS[name])
        if once("weights"):
            for cp in w_copies:
                cp.wait()
        if name != "o" and once("adapter"):
            for k in range(TWIDE - 1):
                arrive(wd.at[(t + TWIDE - 1 - k) % TWIDE, pl.ds(UNITS, RANK)], b_s.at[k], b_r.at[k])
        j = ch[name]
        block = held[j, pl.ds(i * GPART, GPART)].astype(F32)
        xrows = block[:, :CSRC].reshape(ROWS, WIDTH).astype(BF16)
        grows = block[:, CSRC:].reshape(ROWS, WIDTH).astype(BF16)
        first = once(("acc", i))
        for acc, val in ((acc_x, dot(xrows, wgu[j], NT)), (acc_d, dot(grows, wd[j], NT))):
            if first:
                acc[i] = val
            else:
                acc[i] += val

    def middle(i):
        rows = pl.ds(i * ROWS, ROWS)
        probe_i = acc_d[i][:, UNITS:].astype(BF16)
        probe[rows, :] = probe_i
        gate, up = acc_x[i][:, :UNITS], acc_x[i][:, UNITS:]
        dh = acc_d[i][:, :UNITS] + SCALE * dot(probe_i, lead[0])
        sig = jax.nn.sigmoid(gate)
        act = gate * sig
        hidden = (act * up).astype(BF16)
        hid[rows, :] = hidden
        dgate = dh * up * sig * (1.0 + gate * (1.0 - sig))
        dboth[i] = jnp.concatenate([dgate, dh * act], axis=1).astype(BF16)
        low_mine[:, i * ROWS : (i + 1) * ROWS] = dot(lead[0], hidden, NT)

    def sum_send(i, m, val):
        rows = SUMS[m][2]
        sum_out[i, m, 0:rows] = val.astype(BF16)
        send(
            sum_out.at[i, m, pl.ds(0, rows)], sum_in.at[i, m, pl.ds(0, rows)],
            rs_s.at[i, m], rs_r.at[i, m], way[SUMS[m][3]],
        )

    def sum_got(i, m):
        rows = SUMS[m][2]
        arrive(sum_in.at[i, m, pl.ds(0, rows)], rs_s.at[i, m], rs_r.at[i, m])
        return sum_in[i, m, 0:rows].astype(F32)

    def make(i, name):
        val = dot(dboth[i], wgu[ch[name]])
        part_sum[i, NAMES.index(name)] = val
        for m in MAKE[name]:
            sum_send(i, m, val[SUMS[m][1] : SUMS[m][1] + SUMS[m][2]])

    def add_to(val, base, i, m):
        at, n = SUMS[m][1] - base, SUMS[m][2]
        pieces = [val[:at], val[at : at + n] + sum_got(i, m), val[at + n :]]
        return jnp.concatenate([p for p in pieces if p.shape[0]], axis=0)

    def add_step(i, step):
        needs, m = ADDS[step]
        name, at, n, _ = SUMS[m]
        val = part_sum[i, NAMES.index(name), at : at + n]
        for k in needs:
            val = add_to(val, at, i, k)
        sum_send(i, m, val)

    def finish(i):
        val = part_sum[i, NAMES.index("o")]
        for m in LAST:
            val = add_to(val, 0, i, m)
        val = val.reshape(GPART, CSRC, WIDTH)
        ret_out[pl.ds(i * GPART, GPART)] = jnp.concatenate(
            [val[:, :, :512], val[:, :, 384:]], axis=1
        ).astype(BF16)
        for p in range(max(1, i * GPART), (i + 1) * GPART):
            send(ret_out.at[p], ret_in.at[p], ret_s.at[p], ret_r.at[p], expert_at(p, -1))

    def combine(i):
        for p in range(max(1, i * GPART), (i + 1) * GPART):
            arrive(ret_in.at[p], ret_s.at[p], ret_r.at[p])
        if i == 0:
            ret_in[0] = ret_out[0]
        back = ret_in[pl.ds(i * GPART, GPART)].astype(F32)
        first = back[:, :CSRC].reshape(ROWS, 512).astype(BF16)
        last = back[:, CSRC:, 128:].reshape(ROWS, WIDTH - 512).astype(BF16)
        rows = pick[pl.ds(i * ROWS, ROWS), :]
        return jnp.concatenate([dot(rows, first, TN), dot(rows, last, TN)], axis=1)

    def adapters():
        lead_out[0] = SCALE * dot(probe[...], hid[...], TN)
        grows = held[t].astype(F32)[:, CSRC:].reshape(GROUPS * CSRC, WIDTH).astype(BF16)
        low = low_mine[...]
        for k in range(TWIDE - 1):
            arrive(low_all.at[k], low_s.at[k], low_r.at[k])
            low = low + low_all[k]
        trail_out[0] = SCALE * dot(low.astype(BF16), grows)

    for i, step in ORDER:
        if step in STEPS:
            gather_step(i, step)
        elif step in ADDS:
            add_step(i, step)
        elif step == "mid":
            middle(i)
            if i == PARTS - 1:
                for k, peer in enumerate(peers):
                    send(low_mine, low_all.at[k], low_s.at[k], low_r.at[k], peer)
        elif step == "end":
            if i == PARTS - 1:
                adapters()
                mixed[...] = combine(0)
            finish(i)
        elif step[0] == "c":
            products(i, step[1:])
        else:
            make(i, step[1:])

    total = mixed[...]
    for i in range(1, PARTS):
        total = total + combine(i)
    out[...] = total.astype(BF16)

    for cp in started:
        cp.wait_send()


def copy_out(a, b, c, x, y, z):
    x[...] = a[...]
    y[...] = b[...]
    z[...] = c[...]


def on_device(tok, grad, routes, weights, wg, wu, wd, lead, trail):
    vm = pl.BlockSpec(memory_space=pltpu.VMEM)
    hbm = pl.BlockSpec(memory_space=pl.ANY)
    dma = pltpu.SemaphoreType.DMA
    dx, lead_t, trail_t = pl.pallas_call(
        kernel,
        out_shape=(
            jax.ShapeDtypeStruct((64, WIDTH), BF16),
            jax.ShapeDtypeStruct((1, RANK, UNITS), F32),
            jax.ShapeDtypeStruct((1, 16, WIDTH), F32),
        ),
        in_specs=[hbm] * 9,
        out_specs=(vm, vm, vm),
        scratch_shapes=[
            pltpu.VMEM((TWIDE, 2 * UNITS, WIDTH), BF16),
            pltpu.VMEM((TWIDE, UNITS + RANK, WIDTH), BF16),
            pltpu.VMEM((TWIDE, GROUPS, 16, WIDTH), BF16),
            pltpu.VMEM((GROUPS, 16, WIDTH), BF16),
            pltpu.VMEM((PARTS, ROWS, 2 * UNITS), F32),
            pltpu.VMEM((PARTS, ROWS, UNITS + RANK), F32),
            pltpu.VMEM((GROUPS * CSRC, UNITS), BF16),
            pltpu.VMEM((PARTS, ROWS, 2 * UNITS), BF16),
            pltpu.VMEM((GROUPS * CSRC, RANK), BF16),
            pltpu.VMEM((RANK, GROUPS * CSRC), F32),
            pltpu.VMEM((TWIDE - 1, RANK, GROUPS * CSRC), F32),
            pltpu.VMEM((PARTS, TWIDE, ROWS, WIDTH), F32),
            pltpu.VMEM((PARTS, len(SUMS), 32, WIDTH), BF16),
            pltpu.VMEM((PARTS, len(SUMS), 32, WIDTH), BF16),
            pltpu.VMEM((GROUPS, 16, 512), BF16),
            pltpu.VMEM((GROUPS, 16, 512), BF16),
            pltpu.VMEM((GROUPS * CSRC, 64), BF16),
            pltpu.VMEM((64, WIDTH), BF16),
            pltpu.VMEM((64, WIDTH), BF16),
            pltpu.VMEM((2, 64), jnp.int32),
            pltpu.VMEM((2, 64), F32),
            pltpu.VMEM((1, RANK, UNITS), BF16),
            pltpu.VMEM((1, RANK, WIDTH), BF16),
            pltpu.VMEM((64, WIDTH), F32),
            dma((3, TWIDE)),
            dma((GROUPS,)),
            dma((GROUPS,)),
            dma((TWIDE - 1,)),
            dma((TWIDE - 1,)),
            dma((PARTS, len(GATHER))),
            dma((PARTS, len(GATHER))),
            dma((PARTS, len(SUMS))),
            dma((PARTS, len(SUMS))),
            dma((TWIDE - 1,)),
            dma((TWIDE - 1,)),
            dma((GROUPS,)),
            dma((GROUPS,)),
            dma((2,)),
            dma((6,)),
        ],
        compiler_params=pltpu.CompilerParams(
            collective_id=0, has_side_effects=True, vmem_limit_bytes=56 * 1024 * 1024
        ),
        cost_estimate=pl.CostEstimate(
            flops=6_000_000_000, bytes_accessed=16_000_000, transcendentals=80_000
        ),
    )(
        tok, grad, routes.T, weights.T, jnp.swapaxes(wg, 1, 2), jnp.swapaxes(wu, 1, 2),
        wd, jnp.swapaxes(lead, 1, 2), trail,
    )
    results = (dx, lead_t, trail_t)
    dx, lead_t, trail_t = pl.pallas_call(
        copy_out,
        out_shape=tuple(jax.ShapeDtypeStruct(v.shape, v.dtype) for v in results),
        in_specs=[vm] * 3,
        out_specs=(vm,) * 3,
    )(*results)
    return dx, jnp.swapaxes(lead_t, 1, 2), trail_t


def solution(mesh):
    placed = (
        P("expert", "tensor"),
        P("expert", "tensor"),
        P("expert", None),
        P("expert", None),
        P("expert", None, "tensor"),
        P("expert", None, "tensor"),
        P("expert", "tensor", None),
        P("expert", "tensor", None),
        P("expert", None, "tensor"),
    )
    return jax.shard_map(
        on_device,
        mesh=mesh,
        in_specs=placed,
        out_specs=(P("expert", "tensor"), P("expert", "tensor", None), P("expert", None, "tensor")),
        check_vma=False,
    )
```
